32 devices in a mesh: feat: 8 (over y, x, core), rows: 4 (over z).
Axes of the slice: x: 2, y: 2, z: 4, core: 2. Of those that a mesh axis runs over, the one named last changes fastest.
Arguments:
- binned: int32 [8192, 512], P('rows', 'feat'), may hold values from 0 to 255
- node_of: int32 [8192], P('rows'), may hold values from 0 to 31
- margin: float32 [8192], P('rows'), may hold values from -6 to 6
- labels: float32 [8192], P('rows'), may hold values from 0 to 1
- split_feature: int32 [32], replicated, may hold values from 0 to 511
- split_bin: int32 [32], replicated, may hold values from 0 to 255
Outputs:
- histogram: float32 [32, 2, 512, 256], P('rows', None, 'feat')
- margin_out: float32 [8192], P('rows')
- child_out: int32 [8192], P('rows')
- grad_out: float32 [2, 8192], P(None, 'rows')
The draws below stay inside these ranges and needn't reach their ends.
All inputs are finite; a program needn't handle non-finite values.
Results may differ from the reference program's by a relative error of at most 0.0045.
Values may be sent and summed in bfloat16 or wider, within the bound.
A program may use at most 64 MiB of HBM per device.

```python
import jax
import jax.numpy as jnp
from jax import lax

F = 512
BINS = 256
NODES = 32
ROW_DEV = 2048
ROWS = 8192
N_ROWS = 4


def with_ends(array, stream_key, low, largest):
    shape = array.shape
    index_at = [jax.random.randint(jax.random.fold_in(stream_key, axis), (), 0, shape[axis]) for axis in range(len(shape))]
    array = array.at[tuple(index_at)].set(low)
    longest = shape.index(max(shape))
    index_at[longest] = (index_at[longest] + 1) % shape[longest]
    return array.at[tuple(index_at)].set(largest)


def levels(own_key, extent, pieces, least, largest):
    level = 1.0
    for dim, shards_of in pieces:
        steps = jax.random.uniform(jax.random.fold_in(jax.random.fold_in(own_key, 6), dim), (shards_of,), jnp.float32, least / len(pieces), largest / len(pieces))
        level = level * jnp.repeat(jnp.exp(steps), extent[dim] // shards_of).reshape((-1,) + (1,) * (len(extent) - 1 - dim))
    return level


def bell_draw(rng, dims, deviation, limit, split=(), held_as=jnp.bfloat16):
    array = jax.random.normal(rng, dims, jnp.float32) * deviation
    if len(split) > 0:
        array = levels(rng, dims, split, -0.22, 0.18) * array
    return jnp.clip(array, min=-limit, max=limit).astype(held_as)


def setup_inputs(seed: int = 0) -> dict:
    keys = jax.random.split(jax.random.key(seed), 7)
    return {
        "binned": with_ends(jax.random.randint(keys[0], (ROWS, F), 0, BINS), jax.random.fold_in(keys[0], 1), 0, BINS - 1).astype(jnp.int32),
        "node_of": with_ends(jax.random.randint(keys[1], (ROWS,), 0, NODES), jax.random.fold_in(keys[1], 1), 0, NODES - 1).astype(jnp.int32),
        "margin": bell_draw(keys[2], (ROWS,), 1.0, 6.0, ((0, 4),), jnp.float32),
        "labels": jnp.clip(1.0 * jax.random.uniform(keys[3], (ROWS,), jnp.float32) ** levels(keys[3], (ROWS,), ((0, 4),), -0.2, 0.2), 0.0, 1.0),
        "split_feature": with_ends(jax.random.randint(keys[4], (NODES,), 0, F), jax.random.fold_in(keys[4], 1), 0, F - 1).astype(jnp.int32),
        "split_bin": with_ends(jax.random.randint(keys[5], (NODES,), 0, BINS), jax.random.fold_in(keys[5], 1), 0, BINS - 1).astype(jnp.int32),
    }


def leaf_table(selected, split_rows):
    below = (jnp.arange(selected.shape[2])[None, :] <= split_rows[:, None]).astype(jnp.float32)
    left = jnp.sum(selected * below[:, None, :], axis=2)
    whole = jnp.sum(selected, axis=2)
    return jnp.concatenate([left, whole], axis=1)


def reference(binned, node_of, margin, labels, split_feature, split_bin):
    probability = jax.nn.sigmoid(margin)
    gradient = (probability - labels).astype(jnp.bfloat16)
    hessian = (probability * (1.0 - probability)).astype(jnp.bfloat16)
    gradient = lax.optimization_barrier(gradient).astype(jnp.float32)
    hessian = lax.optimization_barrier(hessian).astype(jnp.float32)
    cells = NODES * 2 * F * BINS
    total = jnp.zeros((cells,), jnp.float32)
    feature_ids = jnp.arange(F, dtype=jnp.int32)
    for shard in range(N_ROWS):
        lower = shard * ROW_DEV
        block_bins = binned[lower:lower + ROW_DEV]
        block_nodes = node_of[lower:lower + ROW_DEV]
        for column, values in enumerate((gradient, hessian)):
            index = ((block_nodes[:, None] * 2 + column) * F + feature_ids[None, :]) * BINS + block_bins
            spread = jnp.broadcast_to(values[lower:lower + ROW_DEV][:, None], block_bins.shape)
            part = jax.ops.segment_sum(spread.reshape(-1), index.reshape(-1).astype(jnp.int32), num_segments=cells)
            part = lax.optimization_barrier(part.astype(jnp.bfloat16))
            total = total + part.astype(jnp.float32)
    histogram = total.reshape(NODES, 2, F, BINS)
    selected = histogram[jnp.arange(NODES), :, split_feature, :]
    table = leaf_table(selected, split_bin)
    leaf_left = -table[:, 0] / (table[:, 1] + 1.0)
    leaf_right = -(table[:, 2] - table[:, 0]) / (table[:, 3] - table[:, 1] + 1.0)
    row_feature = split_feature[node_of]
    row_value = jnp.take_along_axis(binned, row_feature[:, None], axis=1)[:, 0]
    go_right = (row_value > split_bin[node_of]).astype(jnp.int32)
    child_out = 2 * node_of + go_right
    margin_out = margin + jnp.where(go_right == 1, leaf_right[node_of], leaf_left[node_of])
    fresh = jax.nn.sigmoid(margin_out)
    grad_out = jnp.stack([fresh - labels, fresh * (1.0 - fresh)], axis=0)
    return histogram, margin_out, child_out, grad_out
```

```python
import functools

import jax
import jax.numpy as jnp
from jax import lax
from jax.experimental import pallas as pl
from jax.experimental.pallas import tpu as pltpu
from jax.sharding import PartitionSpec as P

BINS = 256


def hist_kernel(sources, nodes, feats, raw_ref, out_ref, held, weights, total):
    row_count = raw_ref.shape[2]
    bin_ids = lax.broadcasted_iota(jnp.int32, (BINS, row_count), 0).astype(jnp.bfloat16)
    node_ids = lax.broadcasted_iota(jnp.int32, (2 * nodes, row_count), 0)
    for source in range(sources):
        block = raw_ref[source].astype(jnp.float32)
        held[...] = block
        grad = block[feats : feats + 1]
        hess = block[feats + 1 : feats + 2]
        node = block[feats + 2 : feats + 3].astype(jnp.int32)
        pair = jnp.where(node_ids < nodes, grad, hess)
        mine = jnp.where(node_ids < nodes, node_ids, node_ids - nodes) == node
        weights[...] = jnp.where(mine, pair, 0.0).astype(jnp.bfloat16)

        def add_feature(feat, carry):
            bins = held[pl.ds(feat, 1), :].astype(jnp.bfloat16)
            hot = jnp.where(bin_ids == bins, 1.0, 0.0).astype(jnp.bfloat16)
            piece = lax.dot_general(
                weights[...], hot, (((1,), (1,)), ((), ())), preferred_element_type=jnp.float32
            )
            if source == 0:
                total[feat] = piece
            else:
                total[feat] += piece
            return carry

        lax.fori_loop(0, feats, add_feature, 0)
    out_ref[...] = total[...].astype(out_ref.dtype)


def on_device(binned, node_of, margin, labels, split_feature, split_bin):
    row_count, feat_count = binned.shape
    node_total = split_feature.shape[0]
    sources = lax.axis_size("rows")
    feats = feat_count // sources
    share = node_total // sources
    feat_start = lax.axis_index("feat") * feat_count
    probability = jax.nn.sigmoid(margin)
    gradient = (probability - labels).astype(jnp.bfloat16)
    hessian = (probability * (1.0 - probability)).astype(jnp.bfloat16)
    node_hot = node_of[None, :] == jnp.arange(node_total, dtype=jnp.int32)[:, None]
    row_feature = jnp.sum(jnp.where(node_hot, split_feature[:, None], 0), axis=0)
    row_cut = jnp.sum(jnp.where(node_hot, split_bin[:, None], 0), axis=0)
    local = row_feature - feat_start
    binned_t = binned.T
    column_hot = jnp.arange(feat_count, dtype=jnp.int32)[:, None] == local[None, :]
    right_bits = jnp.sum(
        (column_hot & (binned_t > row_cut[None, :])).astype(jnp.int32), axis=0
    )
    go_right = lax.psum(right_bits, "feat")

    meta = jnp.stack([gradient, hessian, node_of.astype(jnp.bfloat16)], axis=0)
    raw = jnp.concatenate(
        [
            binned_t.astype(jnp.bfloat16).reshape(sources, feats, row_count),
            jnp.broadcast_to(meta[None], (sources, 3, row_count)),
        ],
        axis=1,
    )
    raw = lax.all_to_all(raw, "rows", 0, 0)
    whole = pl.pallas_call(
        functools.partial(hist_kernel, sources, node_total, feats),
        out_shape=jax.ShapeDtypeStruct((feats, 2 * node_total, BINS), jnp.bfloat16),
        in_specs=[pl.BlockSpec(memory_space=pltpu.VMEM)],
        out_specs=pl.BlockSpec(memory_space=pltpu.VMEM),
        scratch_shapes=[
            pltpu.VMEM((feats + 3, row_count), jnp.float32),
            pltpu.VMEM((2 * node_total, row_count), jnp.bfloat16),
            pltpu.VMEM((feats, 2 * node_total, BINS), jnp.float32),
        ],
        compiler_params=pltpu.CompilerParams(vmem_limit_bytes=32 * 1024 * 1024),
    )(raw)
    whole = whole.reshape(feats, 2, sources, share, BINS).transpose(2, 3, 1, 0, 4)
    whole = lax.all_to_all(whole, "rows", 0, 0)
    histogram = whole.transpose(1, 2, 0, 3, 4).reshape(share, 2, feat_count, BINS)
    histogram = histogram.astype(jnp.float32)

    values = jnp.stack([gradient, hessian], axis=0).astype(jnp.float32)
    both = jnp.concatenate([jnp.where(go_right[None, :] == 0, values, 0.0), values], axis=0)
    table = jnp.sum(jnp.where(node_hot[None], both[:, None, :], 0.0), axis=2)
    table = lax.psum(table, "rows")
    leaf_left = -table[0] / (table[1] + 1.0)
    leaf_right = -(table[2] - table[0]) / (table[3] - table[1] + 1.0)
    leaf = jnp.where(go_right[None, :] == 1, leaf_right[:, None], leaf_left[:, None])
    margin_out = margin + jnp.sum(jnp.where(node_hot, leaf, 0.0), axis=0)
    child_out = 2 * node_of + go_right
    fresh = jax.nn.sigmoid(margin_out)
    grad_out = jnp.stack([fresh - labels, fresh * (1.0 - fresh)], axis=0)
    return (histogram, margin_out, child_out, grad_out)


def solution(mesh):
    in_specs = (P("rows", "feat"), P("rows"), P("rows"), P("rows"), P(), P())
    out_specs = (P("rows", None, "feat", None), P("rows"), P("rows"), P(None, "rows"))
    return jax.shard_map(
        on_device, mesh=mesh, in_specs=in_specs, out_specs=out_specs, check_vma=False
    )
```

```python
import functools

import jax
import jax.numpy as jnp
from jax import lax
from jax.experimental import pallas as pl
from jax.experimental.pallas import tpu as pltpu
from jax.sharding import PartitionSpec as P

BINS = 256
GROUP = 4
PAIR = 2
MESH = pl.DeviceIdType.MESH


def level_kernel(
    sources, columns, nodes, feats, bins_ref, meta_ref, bits_ref,
    hist_ref, go_ref, table_ref,
    raw_in, meta_in, bits_in, table_in, held, weights, total, staged,
    raw_send, raw_recv, meta_send, meta_recv, bits_send, bits_recv,
    table_send, table_recv, hist_send, hist_recv,
):
    row_count = bins_ref.shape[2]
    me = lax.axis_index("rows")
    column = lax.axis_index("feat")
    share = 2 * nodes // sources
    groups = feats // GROUP

    def row_peer(step):
        return lax.rem(me + step, sources)

    def feat_peer(step):
        return lax.rem(column + step, columns)

    barrier = pltpu.get_barrier_semaphore()
    for step in range(1, sources):
        pl.semaphore_signal(
            barrier, inc=1, device_id={"rows": row_peer(step)}, device_id_type=MESH
        )

    def greet(step, carry):
        pl.semaphore_signal(
            barrier, inc=1, device_id={"feat": feat_peer(step)}, device_id_type=MESH
        )
        return carry

    lax.fori_loop(1, columns, greet, 0)
    pl.semaphore_wait(barrier, sources - 1 + columns - 1)

    def raw_copy(step, slot, peer):
        return pltpu.make_async_remote_copy(
            src_ref=bins_ref.at[peer], dst_ref=raw_in.at[slot],
            send_sem=raw_send.at[step], recv_sem=raw_recv.at[slot],
            device_id={"rows": peer}, device_id_type=MESH,
        )

    def meta_copy(step, slot, peer):
        return pltpu.make_async_remote_copy(
            src_ref=meta_ref, dst_ref=meta_in.at[slot],
            send_sem=meta_send.at[step], recv_sem=meta_recv.at[slot],
            device_id={"rows": peer}, device_id_type=MESH,
        )

    def bits_copy(step, slot, peer):
        return pltpu.make_async_remote_copy(
            src_ref=bits_ref, dst_ref=bits_in.at[slot],
            send_sem=bits_send.at[step], recv_sem=bits_recv.at[slot],
            device_id={"feat": peer}, device_id_type=MESH,
        )

    def table_copy(step, slot, peer):
        return pltpu.make_async_remote_copy(
            src_ref=table_ref, dst_ref=table_in.at[slot],
            send_sem=table_send.at[step], recv_sem=table_recv.at[slot],
            device_id={"rows": peer}, device_id_type=MESH,
        )

    def hist_copy(step, slot, peer, group):
        part = pl.ds(group * GROUP, GROUP)
        return pltpu.make_async_remote_copy(
            src_ref=staged.at[peer, part], dst_ref=hist_ref.at[slot, part],
            send_sem=hist_send.at[step, group], recv_sem=hist_recv.at[slot, group],
            device_id={"rows": peer}, device_id_type=MESH,
        )

    def send_bits(step, carry):
        bits_copy(step, column, feat_peer(step)).start()
        return carry

    lax.fori_loop(1, columns, send_bits, 0)
    for step in range(1, sources):
        meta_copy(step, me, row_peer(step)).start()
        raw_copy(step, me, row_peer(step)).start()

    bin_ids = lax.broadcasted_iota(jnp.int32, (BINS, row_count), 0)
    cells = lax.broadcasted_iota(jnp.int32, (2 * nodes, row_count), 0)
    cell_node = cells // 2
    is_grad = cells % 2 == 0

    def set_block(bins, meta):
        held[...] = bins.astype(jnp.float32).astype(jnp.int32)
        node = meta[2:3].astype(jnp.int32)
        pair = jnp.where(is_grad, meta[0:1], meta[1:2])
        weights[...] = jnp.where(cell_node == node, pair, 0.0).astype(jnp.bfloat16)

    def piece_of(feat):
        hot = (bin_ids == held[pl.ds(feat, 1), :]).astype(jnp.float32).astype(jnp.bfloat16)
        return lax.dot_general(
            weights[...], hot, (((1,), (1,)), ((), ())), preferred_element_type=jnp.float32
        )

    def add_block(first):
        def add_pair(index, carry):
            for offset in range(PAIR):
                feat = index * PAIR + offset
                if first:
                    total[feat] = piece_of(feat)
                else:
                    total[feat] += piece_of(feat)
            return carry

        lax.fori_loop(0, feats // PAIR, add_pair, 0)

    set_block(bins_ref[me], meta_ref[...])
    add_block(True)

    go_ref[...] = bits_ref[...]

    def take_bits(step, carry):
        peer = feat_peer(step)
        bits_copy(step, peer, peer).wait_recv()
        go_ref[...] += bits_in[peer]
        return carry

    lax.fori_loop(1, columns, take_bits, 0)
    node = meta_ref[2:3].astype(jnp.int32)
    mine = lax.broadcasted_iota(jnp.int32, (nodes, row_count), 0) == node
    left = go_ref[...] == 0
    lanes = lax.broadcasted_iota(jnp.int32, (nodes, 128), 1)
    table = jnp.zeros((nodes, 128), jnp.float32)
    for index in range(4):
        value = meta_ref[index % 2 : index % 2 + 1]
        if index < 2:
            value = jnp.where(left, value, 0.0)
        summed = jnp.sum(jnp.where(mine, value, 0.0), axis=1, keepdims=True)
        table = jnp.where(lanes == index, summed, table)
    table_ref[...] = table
    for step in range(1, sources):
        table_copy(step, me, row_peer(step)).start()

    for step in range(1, sources):
        peer = row_peer(step)
        meta_copy(step, peer, peer).wait_recv()
        raw_copy(step, peer, peer).wait_recv()
        set_block(raw_in[peer], meta_in[peer])
        if step < sources - 1:
            add_block(False)

    def finish(group, carry):
        for offset in range(GROUP):
            feat = group * GROUP + offset
            done = (total[feat] + piece_of(feat)).astype(jnp.bfloat16)
            for dest in range(sources):
                staged[dest, feat] = done[dest * share : (dest + 1) * share]
        for step in range(1, sources):
            hist_copy(step, me, row_peer(step), group).start()
        return carry

    lax.fori_loop(0, groups, finish, 0)
    hist_ref[me] = staged[me]

    def end_bits(step, carry):
        bits_copy(step, column, feat_peer(step)).wait_send()
        return carry

    lax.fori_loop(1, columns, end_bits, 0)
    for step in range(1, sources):
        peer = row_peer(step)
        meta_copy(step, me, peer).wait_send()
        raw_copy(step, me, peer).wait_send()
        table_copy(step, me, peer).wait_send()
    for step in range(1, sources):
        peer = row_peer(step)
        table_copy(step, peer, peer).wait_recv()
        table_ref[...] += table_in[peer]
    for step in range(1, sources):
        peer = row_peer(step)

        def end_group(group, carry):
            hist_copy(step, me, peer, group).wait_send()
            hist_copy(step, peer, peer, group).wait_recv()
            return carry

        lax.fori_loop(0, groups, end_group, 0)


def on_device(binned, node_of, margin, labels, split_feature, split_bin):
    row_count, feat_count = binned.shape
    nodes = split_feature.shape[0]
    sources = lax.axis_size("rows")
    columns = lax.axis_size("feat")
    feats = feat_count // sources
    share = 2 * nodes // sources
    feat_start = lax.axis_index("feat") * feat_count
    probability = jax.nn.sigmoid(margin)
    gradient = (probability - labels).astype(jnp.bfloat16)
    hessian = (probability * (1.0 - probability)).astype(jnp.bfloat16)
    node_hot = node_of[None, :] == jnp.arange(nodes, dtype=jnp.int32)[:, None]
    row_feature = jnp.sum(jnp.where(node_hot, split_feature[:, None], 0), axis=0)
    row_cut = jnp.sum(jnp.where(node_hot, split_bin[:, None], 0), axis=0)
    local = row_feature - feat_start
    binned_t = binned.T
    column_hot = jnp.arange(feat_count, dtype=jnp.int32)[:, None] == local[None, :]
    right_bits = jnp.sum(
        (column_hot & (binned_t > row_cut[None, :])).astype(jnp.int32), axis=0, keepdims=True
    )
    bins = binned_t.astype(jnp.bfloat16).reshape(sources, feats, row_count)
    meta = jnp.stack(
        [gradient.astype(jnp.float32), hessian.astype(jnp.float32), node_of.astype(jnp.float32)]
    )
    vmem = pl.BlockSpec(memory_space=pltpu.VMEM)
    dma = pltpu.SemaphoreType.DMA
    hist, go_right, table = pl.pallas_call(
        functools.partial(level_kernel, sources, columns, nodes, feats),
        out_shape=[
            jax.ShapeDtypeStruct((sources, feats, share, BINS), jnp.bfloat16),
            jax.ShapeDtypeStruct((1, row_count), jnp.int32),
            jax.ShapeDtypeStruct((nodes, 128), jnp.float32),
        ],
        in_specs=[vmem] * 3,
        out_specs=[vmem] * 3,
        scratch_shapes=[
            pltpu.VMEM((sources, feats, row_count), jnp.bfloat16),
            pltpu.VMEM((sources, 3, row_count), jnp.float32),
            pltpu.VMEM((columns, 1, row_count), jnp.int32),
            pltpu.VMEM((sources, nodes, 128), jnp.float32),
            pltpu.VMEM((feats, row_count), jnp.int32),
            pltpu.VMEM((2 * nodes, row_count), jnp.bfloat16),
            pltpu.VMEM((feats, 2 * nodes, BINS), jnp.float32),
            pltpu.VMEM((sources, feats, share, BINS), jnp.bfloat16),
            dma((sources,)),
            dma((sources,)),
            dma((sources,)),
            dma((sources,)),
            dma((columns,)),
            dma((columns,)),
            dma((sources,)),
            dma((sources,)),
            dma((sources, feats // GROUP)),
            dma((sources, feats // GROUP)),
        ],
        compiler_params=pltpu.CompilerParams(
            collective_id=0, has_side_effects=True, vmem_limit_bytes=40 * 1024 * 1024
        ),
    )(bins, meta, right_bits)
    histogram = hist.transpose(2, 0, 1, 3).reshape(nodes // sources, 2, feat_count, BINS)
    histogram = histogram.astype(jnp.float32)

    go_right = go_right[0]
    leaf_left = -table[:, 0] / (table[:, 1] + 1.0)
    leaf_right = -(table[:, 2] - table[:, 0]) / (table[:, 3] - table[:, 1] + 1.0)
    leaf = jnp.where(go_right[None, :] == 1, leaf_right[:, None], leaf_left[:, None])
    margin_out = margin + jnp.sum(jnp.where(node_hot, leaf, 0.0), axis=0)
    child_out = 2 * node_of + go_right
    fresh = jax.nn.sigmoid(margin_out)
    grad_out = jnp.stack([fresh - labels, fresh * (1.0 - fresh)], axis=0)
    return (histogram, margin_out, child_out, grad_out)


def solution(mesh):
    in_specs = (P("rows", "feat"), P("rows"), P("rows"), P("rows"), P(), P())
    out_specs = (P("rows", None, "feat", None), P("rows"), P("rows"), P(None, "rows"))
    return jax.shard_map(
        on_device, mesh=mesh, in_specs=in_specs, out_specs=out_specs, check_vma=False
    )
```

```python
import functools

import jax
import jax.numpy as jnp
from jax import lax
from jax.experimental import pallas as pl
from jax.experimental.pallas import tpu as pltpu
from jax.sharding import PartitionSpec as P

BINS = 256
GROUP = 4
PAIR = 4
SCALE = 256.0
FINE = 16.0
MESH = pl.DeviceIdType.MESH


def level_kernel(
    sources, columns, nodes, feats, bins_ref, meta_ref, bits_ref,
    hist_ref, go_ref, table_ref,
    raw_in, meta_in, bits_in, table_in, held, weights, total, staged,
    raw_send, raw_recv, meta_send, meta_recv, bits_send, bits_recv,
    table_send, table_recv, hist_send, hist_recv,
):
    row_count = bins_ref.shape[2]
    me = lax.axis_index("rows")
    column = lax.axis_index("feat")
    share = 2 * nodes // sources
    groups = feats // GROUP

    def row_peer(step):
        return lax.rem(me + step, sources)

    def feat_peer(step):
        return lax.rem(column + step, columns)

    barrier = pltpu.get_barrier_semaphore()
    for step in range(1, sources):
        pl.semaphore_signal(
            barrier, inc=1, device_id={"rows": row_peer(step)}, device_id_type=MESH
        )

    def greet(step, carry):
        pl.semaphore_signal(
            barrier, inc=1, device_id={"feat": feat_peer(step)}, device_id_type=MESH
        )
        return carry

    lax.fori_loop(1, columns, greet, 0)
    pl.semaphore_wait(barrier, sources - 1 + columns - 1)

    def raw_copy(step, slot, peer):
        return pltpu.make_async_remote_copy(
            src_ref=bins_ref.at[peer], dst_ref=raw_in.at[slot],
            send_sem=raw_send.at[step], recv_sem=raw_recv.at[slot],
            device_id={"rows": peer}, device_id_type=MESH,
        )

    def meta_copy(step, slot, peer):
        return pltpu.make_async_remote_copy(
            src_ref=meta_ref, dst_ref=meta_in.at[slot],
            send_sem=meta_send.at[step], recv_sem=meta_recv.at[slot],
            device_id={"rows": peer}, device_id_type=MESH,
        )

    def bits_copy(step, slot, peer):
        return pltpu.make_async_remote_copy(
            src_ref=bits_ref, dst_ref=bits_in.at[slot],
            send_sem=bits_send.at[step], recv_sem=bits_recv.at[slot],
            device_id={"feat": peer}, device_id_type=MESH,
        )

    def table_copy(step, slot, peer):
        return pltpu.make_async_remote_copy(
            src_ref=table_ref, dst_ref=table_in.at[slot],
            send_sem=table_send.at[step], recv_sem=table_recv.at[slot],
            device_id={"rows": peer}, device_id_type=MESH,
        )

    def hist_copy(step, slot, peer, group):
        part = pl.ds(group * GROUP, GROUP)
        return pltpu.make_async_remote_copy(
            src_ref=staged.at[peer, part], dst_ref=hist_ref.at[slot, part],
            send_sem=hist_send.at[step, group], recv_sem=hist_recv.at[slot, group],
            device_id={"rows": peer}, device_id_type=MESH,
        )

    def send_bits(step, carry):
        bits_copy(step, column, feat_peer(step)).start()
        return carry

    lax.fori_loop(1, columns, send_bits, 0)
    for step in range(1, sources):
        meta_copy(step, me, row_peer(step)).start()
        raw_copy(step, me, row_peer(step)).start()

    bin_ids = lax.broadcasted_iota(jnp.int32, (BINS, row_count), 0).astype(jnp.bfloat16)
    cells = lax.broadcasted_iota(jnp.int32, (2 * nodes, row_count), 0)
    cell_node = cells // 2
    is_grad = cells % 2 == 0

    def set_block(bins, meta):
        held[...] = bins.astype(jnp.float32)
        node = meta[2:3].astype(jnp.int32)
        pair = jnp.where(is_grad, meta[0:1], meta[1:2])
        value = jnp.where(cell_node == node, pair * SCALE, 0.0)
        coarse = value.astype(jnp.float8_e4m3fn)
        rest = (value - coarse.astype(jnp.float32)) * FINE
        weights[: 2 * nodes] = coarse
        weights[2 * nodes :] = rest.astype(jnp.float8_e4m3fn)

    def piece_of(feat):
        bins = held[pl.ds(feat, 1), :].astype(jnp.bfloat16)
        hot = jnp.where(bin_ids == bins, jnp.bfloat16(1), jnp.bfloat16(0))
        hot = hot.astype(jnp.float8_e4m3fn)
        return lax.dot_general(
            weights[...], hot, (((1,), (1,)), ((), ())), preferred_element_type=jnp.float32
        )

    def add_block(first):
        def add_pair(index, carry):
            for offset in range(PAIR):
                feat = index * PAIR + offset
                if first:
                    total[feat] = piece_of(feat)
                else:
                    total[feat] += piece_of(feat)
            return carry

        lax.fori_loop(0, feats // PAIR, add_pair, 0)

    set_block(bins_ref[me], meta_ref[...])
    add_block(True)

    go_ref[...] = bits_ref[...]

    def take_bits(step, carry):
        peer = feat_peer(step)
        bits_copy(step, peer, peer).wait_recv()
        go_ref[...] += bits_in[peer]
        return carry

    lax.fori_loop(1, columns, take_bits, 0)
    node = meta_ref[2:3].astype(jnp.int32)
    mine = lax.broadcasted_iota(jnp.int32, (nodes, row_count), 0) == node
    left = go_ref[...] == 0
    lanes = lax.broadcasted_iota(jnp.int32, (nodes, 128), 1)
    table = jnp.zeros((nodes, 128), jnp.float32)
    for index in range(4):
        value = meta_ref[index % 2 : index % 2 + 1]
        if index < 2:
            value = jnp.where(left, value, 0.0)
        summed = jnp.sum(jnp.where(mine, value, 0.0), axis=1, keepdims=True)
        table = jnp.where(lanes == index, summed, table)
    table_ref[...] = table
    for step in range(1, sources):
        table_copy(step, me, row_peer(step)).start()

    for step in range(1, sources):
        peer = row_peer(step)
        meta_copy(step, peer, peer).wait_recv()
        raw_copy(step, peer, peer).wait_recv()
        set_block(raw_in[peer], meta_in[peer])
        if step < sources - 1:
            add_block(False)

    def finish(group, carry):
        for offset in range(GROUP):
            feat = group * GROUP + offset
            both = total[feat] + piece_of(feat)
            done = both[: 2 * nodes] + both[2 * nodes :] * (1.0 / FINE)
            done = (done * (1.0 / SCALE)).astype(jnp.bfloat16)
            for dest in range(sources):
                staged[dest, feat] = done[dest * share : (dest + 1) * share]
        for step in range(1, sources):
            hist_copy(step, me, row_peer(step), group).start()
        return carry

    lax.fori_loop(0, groups, finish, 0)
    hist_ref[me] = staged[me]

    def end_bits(step, carry):
        bits_copy(step, column, feat_peer(step)).wait_send()
        return carry

    lax.fori_loop(1, columns, end_bits, 0)
    for step in range(1, sources):
        peer = row_peer(step)
        meta_copy(step, me, peer).wait_send()
        raw_copy(step, me, peer).wait_send()
        table_copy(step, me, peer).wait_send()
    for step in range(1, sources):
        peer = row_peer(step)
        table_copy(step, peer, peer).wait_recv()
        table_ref[...] += table_in[peer]
    for step in range(1, sources):
        peer = row_peer(step)

        def end_group(group, carry):
            hist_copy(step, me, peer, group).wait_send()
            hist_copy(step, peer, peer, group).wait_recv()
            return carry

        lax.fori_loop(0, groups, end_group, 0)


def on_device(binned, node_of, margin, labels, split_feature, split_bin):
    row_count, feat_count = binned.shape
    nodes = split_feature.shape[0]
    sources = lax.axis_size("rows")
    columns = lax.axis_size("feat")
    feats = feat_count // sources
    share = 2 * nodes // sources
    feat_start = lax.axis_index("feat") * feat_count
    probability = jax.nn.sigmoid(margin)
    gradient = (probability - labels).astype(jnp.bfloat16)
    hessian = (probability * (1.0 - probability)).astype(jnp.bfloat16)
    node_hot = node_of[None, :] == jnp.arange(nodes, dtype=jnp.int32)[:, None]
    row_feature = jnp.sum(jnp.where(node_hot, split_feature[:, None], 0), axis=0)
    row_cut = jnp.sum(jnp.where(node_hot, split_bin[:, None], 0), axis=0)
    local = row_feature - feat_start
    binned_t = binned.T
    column_hot = jnp.arange(feat_count, dtype=jnp.int32)[:, None] == local[None, :]
    right_bits = jnp.sum(
        (column_hot & (binned_t > row_cut[None, :])).astype(jnp.int32), axis=0, keepdims=True
    )
    bins = binned_t.astype(jnp.bfloat16).reshape(sources, feats, row_count)
    meta = jnp.stack(
        [gradient.astype(jnp.float32), hessian.astype(jnp.float32), node_of.astype(jnp.float32)]
    )
    vmem = pl.BlockSpec(memory_space=pltpu.VMEM)
    dma = pltpu.SemaphoreType.DMA
    hist, go_right, table = pl.pallas_call(
        functools.partial(level_kernel, sources, columns, nodes, feats),
        out_shape=[
            jax.ShapeDtypeStruct((sources, feats, share, BINS), jnp.bfloat16),
            jax.ShapeDtypeStruct((1, row_count), jnp.int32),
            jax.ShapeDtypeStruct((nodes, 128), jnp.float32),
        ],
        in_specs=[vmem] * 3,
        out_specs=[vmem] * 3,
        scratch_shapes=[
            pltpu.VMEM((sources, feats, row_count), jnp.bfloat16),
            pltpu.VMEM((sources, 3, row_count), jnp.float32),
            pltpu.VMEM((columns, 1, row_count), jnp.int32),
            pltpu.VMEM((sources, nodes, 128), jnp.float32),
            pltpu.VMEM((feats, row_count), jnp.float32),
            pltpu.VMEM((4 * nodes, row_count), jnp.float8_e4m3fn),
            pltpu.VMEM((feats, 4 * nodes, BINS), jnp.float32),
            pltpu.VMEM((sources, feats, share, BINS), jnp.bfloat16),
            dma((sources,)),
            dma((sources,)),
            dma((sources,)),
            dma((sources,)),
            dma((columns,)),
            dma((columns,)),
            dma((sources,)),
            dma((sources,)),
            dma((sources, feats // GROUP)),
            dma((sources, feats // GROUP)),
        ],
        compiler_params=pltpu.CompilerParams(
            collective_id=0, has_side_effects=True, vmem_limit_bytes=40 * 1024 * 1024
        ),
    )(bins, meta, right_bits)
    histogram = hist.transpose(2, 0, 1, 3).reshape(nodes // sources, 2, feat_count, BINS)
    histogram = histogram.astype(jnp.float32)

    go_right = go_right[0]
    leaf_left = -table[:, 0] / (table[:, 1] + 1.0)
    leaf_right = -(table[:, 2] - table[:, 0]) / (table[:, 3] - table[:, 1] + 1.0)
    leaf = jnp.where(go_right[None, :] == 1, leaf_right[:, None], leaf_left[:, None])
    margin_out = margin + jnp.sum(jnp.where(node_hot, leaf, 0.0), axis=0)
    child_out = 2 * node_of + go_right
    fresh = jax.nn.sigmoid(margin_out)
    grad_out = jnp.stack([fresh - labels, fresh * (1.0 - fresh)], axis=0)
    return (histogram, margin_out, child_out, grad_out)


def solution(mesh):
    in_specs = (P("rows", "feat"), P("rows"), P("rows"), P("rows"), P(), P())
    out_specs = (P("rows", None, "feat", None), P("rows"), P("rows"), P(None, "rows"))
    return jax.shard_map(
        on_device, mesh=mesh, in_specs=in_specs, out_specs=out_specs, check_vma=False
    )
```

```python
import functools

import jax
import jax.numpy as jnp
from jax import lax
from jax.experimental import pallas as pl
from jax.experimental.pallas import tpu as pltpu
from jax.sharding import PartitionSpec as P

BINS = 256
GROUP = 4
PAIR = 4
SCALE = 256.0
FINE = 16.0
MESH = pl.DeviceIdType.MESH


def level_kernel(
    sources, columns, nodes, feats, bins_ref, meta_ref, bits_ref,
    hist_ref, go_ref, table_ref,
    raw_in, meta_in, bits_in, table_in, held, weights, total, staged,
    raw_send, raw_recv, meta_send, meta_recv, bits_send, bits_recv,
    table_send, table_recv, hist_send, hist_recv,
):
    row_count = bins_ref.shape[2]
    me = lax.axis_index("rows")
    column = lax.axis_index("feat")
    share = 2 * nodes // sources
    groups = feats // GROUP
    last = range(max(1, sources - 2), sources)

    def row_peer(step):
        return lax.rem(me + step, sources)

    def feat_peer(step):
        return lax.rem(column + step, columns)

    barrier = pltpu.get_barrier_semaphore()
    for step in range(1, sources):
        pl.semaphore_signal(
            barrier, inc=1, device_id={"rows": row_peer(step)}, device_id_type=MESH
        )

    def greet(step, carry):
        pl.semaphore_signal(
            barrier, inc=1, device_id={"feat": feat_peer(step)}, device_id_type=MESH
        )
        return carry

    lax.fori_loop(1, columns, greet, 0)
    bin_ids = lax.broadcasted_iota(jnp.int32, (BINS, row_count), 0).astype(jnp.bfloat16)
    cells = lax.broadcasted_iota(jnp.int32, (2 * nodes, row_count), 0)
    cell_node = cells // 2
    is_grad = cells % 2 == 0

    def set_block(step, bins, meta):
        held[step] = bins.astype(jnp.float32)
        node = meta[2:3].astype(jnp.int32)
        pair = jnp.where(is_grad, meta[0:1], meta[1:2])
        value = jnp.where(cell_node == node, pair * SCALE, 0.0)
        coarse = value.astype(jnp.float8_e4m3fn)
        rest = (value - coarse.astype(jnp.float32)) * FINE
        weights[step, : 2 * nodes] = coarse
        weights[step, 2 * nodes :] = rest.astype(jnp.float8_e4m3fn)

    def piece_of(step, feat):
        bins = held[step, pl.ds(feat, 1), :].astype(jnp.bfloat16)
        hot = jnp.where(bin_ids == bins, jnp.bfloat16(1), jnp.bfloat16(0))
        hot = hot.astype(jnp.float8_e4m3fn)
        return lax.dot_general(
            weights[step], hot, (((1,), (1,)), ((), ())), preferred_element_type=jnp.float32
        )

    def add_block(step):
        def add_pair(index, carry):
            for offset in range(PAIR):
                feat = index * PAIR + offset
                if step == 0:
                    total[feat] = piece_of(step, feat)
                else:
                    total[feat] += piece_of(step, feat)
            return carry

        lax.fori_loop(0, feats // PAIR, add_pair, 0)

    set_block(0, bins_ref[me], meta_ref[...])
    pl.semaphore_wait(barrier, sources - 1 + columns - 1)

    def raw_copy(step, slot, peer):
        return pltpu.make_async_remote_copy(
            src_ref=bins_ref.at[peer], dst_ref=raw_in.at[slot],
            send_sem=raw_send.at[step], recv_sem=raw_recv.at[slot],
            device_id={"rows": peer}, device_id_type=MESH,
        )

    def meta_copy(step, slot, peer):
        return pltpu.make_async_remote_copy(
            src_ref=meta_ref, dst_ref=meta_in.at[slot],
            send_sem=meta_send.at[step], recv_sem=meta_recv.at[slot],
            device_id={"rows": peer}, device_id_type=MESH,
        )

    def bits_copy(step, slot, peer):
        return pltpu.make_async_remote_copy(
            src_ref=bits_ref, dst_ref=bits_in.at[slot],
            send_sem=bits_send.at[step], recv_sem=bits_recv.at[slot],
            device_id={"feat": peer}, device_id_type=MESH,
        )

    def table_copy(step, slot, peer):
        return pltpu.make_async_remote_copy(
            src_ref=table_ref, dst_ref=table_in.at[slot],
            send_sem=table_send.at[step], recv_sem=table_recv.at[slot],
            device_id={"rows": peer}, device_id_type=MESH,
        )

    def hist_copy(step, slot, peer, group):
        part = pl.ds(group * GROUP, GROUP)
        return pltpu.make_async_remote_copy(
            src_ref=staged.at[peer, part], dst_ref=hist_ref.at[slot, part],
            send_sem=hist_send.at[step, group], recv_sem=hist_recv.at[slot, group],
            device_id={"rows": peer}, device_id_type=MESH,
        )

    def send_bits(step, carry):
        bits_copy(step, column, feat_peer(step)).start()
        return carry

    lax.fori_loop(1, columns, send_bits, 0)
    for step in range(1, sources):
        meta_copy(step, me, row_peer(step)).start()
        raw_copy(step, me, row_peer(step)).start()

    add_block(0)

    go_ref[...] = bits_ref[...]

    def take_bits(step, carry):
        peer = feat_peer(step)
        bits_copy(step, peer, peer).wait_recv()
        go_ref[...] += bits_in[peer]
        return carry

    lax.fori_loop(1, columns, take_bits, 0)
    node = meta_ref[2:3].astype(jnp.int32)
    mine = lax.broadcasted_iota(jnp.int32, (nodes, row_count), 0) == node
    left = go_ref[...] == 0
    lanes = lax.broadcasted_iota(jnp.int32, (nodes, 128), 1)
    table = jnp.zeros((nodes, 128), jnp.float32)
    for index in range(4):
        value = meta_ref[index % 2 : index % 2 + 1]
        if index < 2:
            value = jnp.where(left, value, 0.0)
        summed = jnp.sum(jnp.where(mine, value, 0.0), axis=1, keepdims=True)
        table = jnp.where(lanes == index, summed, table)
    table_ref[...] = table
    for step in range(1, sources):
        table_copy(step, me, row_peer(step)).start()

    for step in range(1, sources):
        peer = row_peer(step)
        meta_copy(step, peer, peer).wait_recv()
        raw_copy(step, peer, peer).wait_recv()
        set_block(step, raw_in[peer], meta_in[peer])
        if step not in last:
            add_block(step)

    def finish(group, carry):
        for offset in range(GROUP):
            feat = group * GROUP + offset
            both = total[feat]
            for step in last:
                both += piece_of(step, feat)
            done = both[: 2 * nodes] + both[2 * nodes :] * (1.0 / FINE)
            done = (done * (1.0 / SCALE)).astype(jnp.bfloat16)
            for dest in range(sources):
                staged[dest, feat] = done[dest * share : (dest + 1) * share]
        for step in range(1, sources):
            hist_copy(step, me, row_peer(step), group).start()
        return carry

    lax.fori_loop(0, groups, finish, 0)
    hist_ref[me] = staged[me]

    def end_bits(step, carry):
        bits_copy(step, column, feat_peer(step)).wait_send()
        return carry

    lax.fori_loop(1, columns, end_bits, 0)
    for step in range(1, sources):
        peer = row_peer(step)
        meta_copy(step, me, peer).wait_send()
        raw_copy(step, me, peer).wait_send()
        table_copy(step, me, peer).wait_send()
    for step in range(1, sources):
        peer = row_peer(step)
        table_copy(step, peer, peer).wait_recv()
        table_ref[...] += table_in[peer]
    for step in range(1, sources):
        peer = row_peer(step)

        def end_group(group, carry):
            hist_copy(step, me, peer, group).wait_send()
            hist_copy(step, peer, peer, group).wait_recv()
            return carry

        lax.fori_loop(0, groups, end_group, 0)


def on_device(binned, node_of, margin, labels, split_feature, split_bin):
    row_count, feat_count = binned.shape
    nodes = split_feature.shape[0]
    sources = lax.axis_size("rows")
    columns = lax.axis_size("feat")
    feats = feat_count // sources
    share = 2 * nodes // sources
    feat_start = lax.axis_index("feat") * feat_count
    probability = jax.nn.sigmoid(margin)
    gradient = lax.reduce_precision(probability - labels, 8, 7)
    hessian = lax.reduce_precision(probability * (1.0 - probability), 8, 7)
    node_hot = node_of[None, :] == jnp.arange(nodes, dtype=jnp.int32)[:, None]
    row_feature = jnp.sum(jnp.where(node_hot, split_feature[:, None], 0), axis=0)
    row_cut = jnp.sum(jnp.where(node_hot, split_bin[:, None], 0), axis=0)
    local = row_feature - feat_start
    binned_t = binned.T
    column_hot = jnp.arange(feat_count, dtype=jnp.int32)[:, None] == local[None, :]
    right_bits = jnp.sum(
        (column_hot & (binned_t > row_cut[None, :])).astype(jnp.int32), axis=0, keepdims=True
    )
    bins = binned_t.astype(jnp.bfloat16).reshape(sources, feats, row_count)
    meta = jnp.stack([gradient, hessian, node_of.astype(jnp.float32)])
    vmem = pl.BlockSpec(memory_space=pltpu.VMEM)
    dma = pltpu.SemaphoreType.DMA
    hist, go_right, table = pl.pallas_call(
        functools.partial(level_kernel, sources, columns, nodes, feats),
        out_shape=[
            jax.ShapeDtypeStruct((sources, feats, share, BINS), jnp.bfloat16),
            jax.ShapeDtypeStruct((1, row_count), jnp.int32),
            jax.ShapeDtypeStruct((nodes, 128), jnp.float32),
        ],
        in_specs=[vmem] * 3,
        out_specs=[vmem] * 3,
        scratch_shapes=[
            pltpu.VMEM((sources, feats, row_count), jnp.bfloat16),
            pltpu.VMEM((sources, 3, row_count), jnp.float32),
            pltpu.VMEM((columns, 1, row_count), jnp.int32),
            pltpu.VMEM((sources, nodes, 128), jnp.float32),
            pltpu.VMEM((sources, feats, row_count), jnp.float32),
            pltpu.VMEM((sources, 4 * nodes, row_count), jnp.float8_e4m3fn),
            pltpu.VMEM((feats, 4 * nodes, BINS), jnp.float32),
            pltpu.VMEM((sources, feats, share, BINS), jnp.bfloat16),
            dma((sources,)),
            dma((sources,)),
            dma((sources,)),
            dma((sources,)),
            dma((columns,)),
            dma((columns,)),
            dma((sources,)),
            dma((sources,)),
            dma((sources, feats // GROUP)),
            dma((sources, feats // GROUP)),
        ],
        compiler_params=pltpu.CompilerParams(
            collective_id=0, has_side_effects=True, vmem_limit_bytes=40 * 1024 * 1024
        ),
    )(bins, meta, right_bits)
    histogram = hist.transpose(2, 0, 1, 3).reshape(nodes // sources, 2, feat_count, BINS)
    histogram = histogram.astype(jnp.float32)

    go_right = go_right[0]
    leaf_left = -table[:, 0] / (table[:, 1] + 1.0)
    leaf_right = -(table[:, 2] - table[:, 0]) / (table[:, 3] - table[:, 1] + 1.0)
    leaf = jnp.where(go_right[None, :] == 1, leaf_right[:, None], leaf_left[:, None])
    margin_out = margin + jnp.sum(jnp.where(node_hot, leaf, 0.0), axis=0)
    child_out = 2 * node_of + go_right
    fresh = jax.nn.sigmoid(margin_out)
    grad_out = jnp.stack([fresh - labels, fresh * (1.0 - fresh)], axis=0)
    return (histogram, margin_out, child_out, grad_out)


def solution(mesh):
    in_specs = (P("rows", "feat"), P("rows"), P("rows"), P("rows"), P(), P())
    out_specs = (P("rows", None, "feat", None), P("rows"), P("rows"), P(None, "rows"))
    return jax.shard_map(
        on_device, mesh=mesh, in_specs=in_specs, out_specs=out_specs, check_vma=False
    )
```

```python
import functools

import jax
import jax.numpy as jnp
from jax import lax
from jax.experimental import pallas as pl
from jax.experimental.pallas import tpu as pltpu
from jax.sharding import PartitionSpec as P

BINS = 256
GROUP = 2
PAIR = 4
SCALE = 256.0
FINE = 16.0
MESH = pl.DeviceIdType.MESH


def level_kernel(
    sources, columns, nodes, feats, bins_ref, meta_ref, bits_ref,
    hist_ref, go_ref, table_ref,
    raw_in, meta_in, bits_in, table_in, held, weights, total, staged,
    raw_send, raw_recv, meta_send, meta_recv, bits_send, bits_recv,
    table_send, table_recv, hist_send, hist_recv,
):
    row_count = bins_ref.shape[2]
    me = lax.axis_index("rows")
    column = lax.axis_index("feat")
    share = 2 * nodes // sources
    groups = feats // GROUP
    last = range(max(1, sources - 2), sources)

    def row_peer(step):
        return lax.rem(me + step, sources)

    def feat_peer(step):
        return lax.rem(column + step, columns)

    barrier = pltpu.get_barrier_semaphore()
    for step in range(1, sources):
        pl.semaphore_signal(
            barrier, inc=1, device_id={"rows": row_peer(step)}, device_id_type=MESH
        )

    def greet(step, carry):
        pl.semaphore_signal(
            barrier, inc=1, device_id={"feat": feat_peer(step)}, device_id_type=MESH
        )
        return carry

    lax.fori_loop(1, columns, greet, 0)
    bin_ids = lax.broadcasted_iota(jnp.int32, (BINS, row_count), 0).astype(jnp.bfloat16)
    cells = lax.broadcasted_iota(jnp.int32, (2 * nodes, row_count), 0)
    cell_node = cells // 2
    is_grad = cells % 2 == 0

    def set_block(step, bins, meta):
        held[step] = bins.astype(jnp.float32)
        node = meta[2:3].astype(jnp.int32)
        pair = jnp.where(is_grad, meta[0:1], meta[1:2])
        value = jnp.where(cell_node == node, pair * SCALE, 0.0)
        coarse = value.astype(jnp.float8_e4m3fn)
        rest = (value - coarse.astype(jnp.float32)) * FINE
        weights[step, : 2 * nodes] = coarse
        weights[step, 2 * nodes :] = rest.astype(jnp.float8_e4m3fn)

    def piece_of(step, feat):
        bins = held[step, pl.ds(feat, 1), :].astype(jnp.bfloat16)
        hot = jnp.where(bin_ids == bins, jnp.bfloat16(1), jnp.bfloat16(0))
        hot = hot.astype(jnp.float8_e4m3fn)
        return lax.dot_general(
            weights[step], hot, (((1,), (1,)), ((), ())), preferred_element_type=jnp.float32
        )

    def add_block(step):
        def add_pair(index, carry):
            for offset in range(PAIR):
                feat = index * PAIR + offset
                if step == 0:
                    total[feat] = piece_of(step, feat)
                else:
                    total[feat] += piece_of(step, feat)
            return carry

        lax.fori_loop(0, feats // PAIR, add_pair, 0)

    set_block(0, bins_ref[me], meta_ref[...])
    pl.semaphore_wait(barrier, sources - 1 + columns - 1)

    def raw_copy(step, slot, peer):
        return pltpu.make_async_remote_copy(
            src_ref=bins_ref.at[peer], dst_ref=raw_in.at[slot],
            send_sem=raw_send.at[step], recv_sem=raw_recv.at[slot],
            device_id={"rows": peer}, device_id_type=MESH,
        )

    def meta_copy(step, slot, peer):
        return pltpu.make_async_remote_copy(
            src_ref=meta_ref, dst_ref=meta_in.at[slot],
            send_sem=meta_send.at[step], recv_sem=meta_recv.at[slot],
            device_id={"rows": peer}, device_id_type=MESH,
        )

    def bits_copy(step, slot, peer):
        return pltpu.make_async_remote_copy(
            src_ref=bits_ref, dst_ref=bits_in.at[slot],
            send_sem=bits_send.at[step], recv_sem=bits_recv.at[slot],
            device_id={"feat": peer}, device_id_type=MESH,
        )

    def table_copy(step, slot, peer):
        return pltpu.make_async_remote_copy(
            src_ref=table_ref, dst_ref=table_in.at[slot],
            send_sem=table_send.at[step], recv_sem=table_recv.at[slot],
            device_id={"rows": peer}, device_id_type=MESH,
        )

    def hist_copy(step, slot, peer, group):
        part = pl.ds(group * GROUP, GROUP)
        return pltpu.make_async_remote_copy(
            src_ref=staged.at[peer, part], dst_ref=hist_ref.at[slot, part],
            send_sem=hist_send.at[step, group], recv_sem=hist_recv.at[slot, group],
            device_id={"rows": peer}, device_id_type=MESH,
        )

    def send_bits(step, carry):
        bits_copy(step, column, feat_peer(step)).start()
        return carry

    lax.fori_loop(1, columns, send_bits, 0)
    for step in range(1, sources):
        meta_copy(step, me, row_peer(step)).start()
        raw_copy(step, me, row_peer(step)).start()

    add_block(0)

    go_ref[...] = bits_ref[...]

    def take_bits(step, carry):
        peer = feat_peer(step)
        bits_copy(step, peer, peer).wait_recv()
        go_ref[...] += bits_in[peer]
        return carry

    lax.fori_loop(1, columns, take_bits, 0)
    node = meta_ref[2:3].astype(jnp.int32)
    mine = lax.broadcasted_iota(jnp.int32, (nodes, row_count), 0) == node
    left = go_ref[...] == 0
    lanes = lax.broadcasted_iota(jnp.int32, (nodes, 128), 1)
    table = jnp.zeros((nodes, 128), jnp.float32)
    for index in range(4):
        value = meta_ref[index % 2 : index % 2 + 1]
        if index < 2:
            value = jnp.where(left, value, 0.0)
        summed = jnp.sum(jnp.where(mine, value, 0.0), axis=1, keepdims=True)
        table = jnp.where(lanes == index, summed, table)
    table_ref[...] = table
    for step in range(1, sources):
        table_copy(step, me, row_peer(step)).start()

    for step in range(1, sources):
        peer = row_peer(step)
        meta_copy(step, peer, peer).wait_recv()
        raw_copy(step, peer, peer).wait_recv()
        set_block(step, raw_in[peer], meta_in[peer])
        if step not in last:
            add_block(step)

    def finish(group, carry):
        for offset in range(GROUP):
            feat = group * GROUP + offset
            both = total[feat]
            for step in last:
                both += piece_of(step, feat)
            done = both[: 2 * nodes] + both[2 * nodes :] * (1.0 / FINE)
            done = (done * (1.0 / SCALE)).astype(jnp.bfloat16)
            for dest in range(sources):
                staged[dest, feat] = done[dest * share : (dest + 1) * share]
        for step in range(1, sources):
            hist_copy(step, me, row_peer(step), group).start()
        return carry

    lax.fori_loop(0, groups, finish, 0)
    hist_ref[me] = staged[me]

    def end_bits(step, carry):
        bits_copy(step, column, feat_peer(step)).wait_send()
        return carry

    lax.fori_loop(1, columns, end_bits, 0)
    for step in range(1, sources):
        peer = row_peer(step)
        meta_copy(step, me, peer).wait_send()
        raw_copy(step, me, peer).wait_send()
        table_copy(step, me, peer).wait_send()
    for step in range(1, sources):
        peer = row_peer(step)
        table_copy(step, peer, peer).wait_recv()
        table_ref[...] += table_in[peer]
    for step in range(1, sources):
        peer = row_peer(step)

        def end_group(group, carry):
            hist_copy(step, me, peer, group).wait_send()
            hist_copy(step, peer, peer, group).wait_recv()
            return carry

        lax.fori_loop(0, groups, end_group, 0)


def on_device(binned, node_of, margin, labels, split_feature, split_bin):
    row_count, feat_count = binned.shape
    nodes = split_feature.shape[0]
    sources = lax.axis_size("rows")
    columns = lax.axis_size("feat")
    feats = feat_count // sources
    share = 2 * nodes // sources
    feat_start = lax.axis_index("feat") * feat_count
    probability = jax.nn.sigmoid(margin)
    gradient = lax.reduce_precision(probability - labels, 8, 7)
    hessian = lax.reduce_precision(probability * (1.0 - probability), 8, 7)
    node_hot = node_of[None, :] == jnp.arange(nodes, dtype=jnp.int32)[:, None]
    row_feature = jnp.sum(jnp.where(node_hot, split_feature[:, None], 0), axis=0)
    row_cut = jnp.sum(jnp.where(node_hot, split_bin[:, None], 0), axis=0)
    local = row_feature - feat_start
    binned_t = binned.T
    column_hot = jnp.arange(feat_count, dtype=jnp.int32)[:, None] == local[None, :]
    right_bits = jnp.sum(
        (column_hot & (binned_t > row_cut[None, :])).astype(jnp.int32), axis=0, keepdims=True
    )
    bins = binned_t.astype(jnp.bfloat16).reshape(sources, feats, row_count)
    meta = jnp.stack([gradient, hessian, node_of.astype(jnp.float32)])
    vmem = pl.BlockSpec(memory_space=pltpu.VMEM)
    dma = pltpu.SemaphoreType.DMA
    hist, go_right, table = pl.pallas_call(
        functools.partial(level_kernel, sources, columns, nodes, feats),
        out_shape=[
            jax.ShapeDtypeStruct((sources, feats, share, BINS), jnp.bfloat16),
            jax.ShapeDtypeStruct((1, row_count), jnp.int32),
            jax.ShapeDtypeStruct((nodes, 128), jnp.float32),
        ],
        in_specs=[vmem] * 3,
        out_specs=[vmem] * 3,
        scratch_shapes=[
            pltpu.VMEM((sources, feats, row_count), jnp.bfloat16),
            pltpu.VMEM((sources, 3, row_count), jnp.float32),
            pltpu.VMEM((columns, 1, row_count), jnp.int32),
            pltpu.VMEM((sources, nodes, 128), jnp.float32),
            pltpu.VMEM((sources, feats, row_count), jnp.float32),
            pltpu.VMEM((sources, 4 * nodes, row_count), jnp.float8_e4m3fn),
            pltpu.VMEM((feats, 4 * nodes, BINS), jnp.float32),
            pltpu.VMEM((sources, feats, share, BINS), jnp.bfloat16),
            dma((sources,)),
            dma((sources,)),
            dma((sources,)),
            dma((sources,)),
            dma((columns,)),
            dma((columns,)),
            dma((sources,)),
            dma((sources,)),
            dma((sources, feats // GROUP)),
            dma((sources, feats // GROUP)),
        ],
        compiler_params=pltpu.CompilerParams(
            collective_id=0, has_side_effects=True, vmem_limit_bytes=40 * 1024 * 1024
        ),
    )(bins, meta, right_bits)
    histogram = hist.transpose(2, 0, 1, 3).reshape(nodes // sources, 2, feat_count, BINS)
    histogram = histogram.astype(jnp.float32)

    go_right = go_right[0]
    leaf_left = -table[:, 0] / (table[:, 1] + 1.0)
    leaf_right = -(table[:, 2] - table[:, 0]) / (table[:, 3] - table[:, 1] + 1.0)
    leaf = jnp.where(go_right[None, :] == 1, leaf_right[:, None], leaf_left[:, None])
    margin_out = margin + jnp.sum(jnp.where(node_hot, leaf, 0.0), axis=0)
    child_out = 2 * node_of + go_right
    fresh = jax.nn.sigmoid(margin_out)
    grad_out = jnp.stack([fresh - labels, fresh * (1.0 - fresh)], axis=0)
    return (histogram, margin_out, child_out, grad_out)


def solution(mesh):
    in_specs = (P("rows", "feat"), P("rows"), P("rows"), P("rows"), P(), P())
    out_specs = (P("rows", None, "feat", None), P("rows"), P("rows"), P(None, "rows"))
    return jax.shard_map(
        on_device, mesh=mesh, in_specs=in_specs, out_specs=out_specs, check_vma=False
    )
```

```python
import functools

import jax
import jax.numpy as jnp
from jax import lax
from jax.experimental import pallas as pl
from jax.experimental.pallas import tpu as pltpu
from jax.sharding import PartitionSpec as P

BINS = 256
GROUP = 2
PAIR = 4
SCALE = 256.0
FINE = 16.0
MESH = pl.DeviceIdType.MESH


def level_kernel(
    sources, columns, nodes, feats, bins_ref, meta_ref, bits_ref,
    hist_ref, go_ref, table_ref,
    raw_in, meta_in, bits_in, table_in, held, weights, total, staged,
    raw_send, raw_recv, meta_send, meta_recv, bits_send, bits_recv,
    table_send, table_recv, hist_send, hist_recv,
):
    row_count = bins_ref.shape[2]
    me = lax.axis_index("rows")
    column = lax.axis_index("feat")
    share = 2 * nodes // sources
    groups = feats // GROUP
    last = range(max(1, sources - 2), sources)

    def row_peer(step):
        return lax.rem(me + step, sources)

    def feat_peer(step):
        return lax.rem(column + step, columns)

    barrier = pltpu.get_barrier_semaphore()
    for step in range(1, sources):
        pl.semaphore_signal(
            barrier, inc=1, device_id={"rows": row_peer(step)}, device_id_type=MESH
        )

    def greet(step, carry):
        pl.semaphore_signal(
            barrier, inc=1, device_id={"feat": feat_peer(step)}, device_id_type=MESH
        )
        return carry

    lax.fori_loop(1, columns, greet, 0)
    bin_ids = lax.broadcasted_iota(jnp.int32, (BINS, row_count), 0).astype(jnp.bfloat16)
    cells = lax.broadcasted_iota(jnp.int32, (2 * nodes, row_count), 0)
    cell_node = cells // 2
    is_grad = cells % 2 == 0

    def set_block(step, bins, meta):
        held[step] = bins.astype(jnp.float32)
        node = meta[2:3].astype(jnp.int32)
        pair = jnp.where(is_grad, meta[0:1], meta[1:2])
        value = jnp.where(cell_node == node, pair * SCALE, 0.0)
        coarse = value.astype(jnp.float8_e4m3fn)
        rest = (value - coarse.astype(jnp.float32)) * FINE
        weights[step, : 2 * nodes] = coarse
        weights[step, 2 * nodes :] = rest.astype(jnp.float8_e4m3fn)

    def piece_of(step, feat):
        bins = held[step, pl.ds(feat, 1), :].astype(jnp.bfloat16)
        hot = jnp.where(bin_ids == bins, jnp.bfloat16(1), jnp.bfloat16(0))
        hot = hot.astype(jnp.float8_e4m3fn)
        return lax.dot_general(
            weights[step], hot, (((1,), (1,)), ((), ())), preferred_element_type=jnp.float32
        )

    def add_block(step):
        def add_pair(index, carry):
            for offset in range(PAIR):
                feat = index * PAIR + offset
                if step == 0:
                    total[feat] = piece_of(step, feat)
                else:
                    total[feat] += piece_of(step, feat)
            return carry

        lax.fori_loop(0, feats // PAIR, add_pair, 0)

    set_block(0, bins_ref[me], meta_ref[...])
    pl.semaphore_wait(barrier, sources - 1 + columns - 1)

    def raw_copy(step, slot, peer):
        return pltpu.make_async_remote_copy(
            src_ref=bins_ref.at[peer], dst_ref=raw_in.at[slot],
            send_sem=raw_send.at[step], recv_sem=raw_recv.at[slot],
            device_id={"rows": peer}, device_id_type=MESH,
        )

    def meta_copy(step, slot, peer):
        return pltpu.make_async_remote_copy(
            src_ref=meta_ref, dst_ref=meta_in.at[slot],
            send_sem=meta_send.at[step], recv_sem=meta_recv.at[slot],
            device_id={"rows": peer}, device_id_type=MESH,
        )

    def bits_copy(step, slot, peer):
        return pltpu.make_async_remote_copy(
            src_ref=bits_ref, dst_ref=bits_in.at[slot],
            send_sem=bits_send.at[step], recv_sem=bits_recv.at[slot],
            device_id={"feat": peer}, device_id_type=MESH,
        )

    def table_copy(step, slot, peer):
        return pltpu.make_async_remote_copy(
            src_ref=table_ref, dst_ref=table_in.at[slot],
            send_sem=table_send.at[step], recv_sem=table_recv.at[slot],
            device_id={"rows": peer}, device_id_type=MESH,
        )

    def hist_copy(step, slot, peer, group):
        part = pl.ds(group * GROUP, GROUP)
        return pltpu.make_async_remote_copy(
            src_ref=staged.at[peer, part], dst_ref=hist_ref.at[slot, part],
            send_sem=hist_send.at[step, group], recv_sem=hist_recv.at[slot, group],
            device_id={"rows": peer}, device_id_type=MESH,
        )

    def send_bits(step, carry):
        bits_copy(step, column, feat_peer(step)).start()
        return carry

    for step in range(1, sources):
        meta_copy(step, me, row_peer(step)).start()
        raw_copy(step, me, row_peer(step)).start()
    lax.fori_loop(1, columns, send_bits, 0)

    add_block(0)

    go_ref[...] = bits_ref[...]

    def take_bits(step, carry):
        peer = feat_peer(step)
        bits_copy(step, peer, peer).wait_recv()
        go_ref[...] += bits_in[peer]
        return carry

    lax.fori_loop(1, columns, take_bits, 0)
    node = meta_ref[2:3].astype(jnp.int32)
    mine = lax.broadcasted_iota(jnp.int32, (nodes, row_count), 0) == node
    left = go_ref[...] == 0
    lanes = lax.broadcasted_iota(jnp.int32, (nodes, 128), 1)
    table = jnp.zeros((nodes, 128), jnp.float32)
    for index in range(4):
        value = meta_ref[index % 2 : index % 2 + 1]
        if index < 2:
            value = jnp.where(left, value, 0.0)
        summed = jnp.sum(jnp.where(mine, value, 0.0), axis=1, keepdims=True)
        table = jnp.where(lanes == index, summed, table)
    table_ref[...] = table
    for step in range(1, sources):
        table_copy(step, me, row_peer(step)).start()

    for step in range(1, sources):
        peer = row_peer(step)
        meta_copy(step, peer, peer).wait_recv()
        raw_copy(step, peer, peer).wait_recv()
        set_block(step, raw_in[peer], meta_in[peer])
        if step not in last:
            add_block(step)

    def finish(group, carry):
        for offset in range(GROUP):
            feat = group * GROUP + offset
            both = total[feat]
            for step in last:
                both += piece_of(step, feat)
            done = both[: 2 * nodes] + both[2 * nodes :] * (1.0 / FINE)
            done = (done * (1.0 / SCALE)).astype(jnp.bfloat16)
            for dest in range(sources):
                staged[dest, feat] = done[dest * share : (dest + 1) * share]
        for step in range(1, sources):
            hist_copy(step, me, row_peer(step), group).start()
        return carry

    lax.fori_loop(0, groups, finish, 0)
    hist_ref[me] = staged[me]

    def end_bits(step, carry):
        bits_copy(step, column, feat_peer(step)).wait_send()
        return carry

    lax.fori_loop(1, columns, end_bits, 0)
    for step in range(1, sources):
        peer = row_peer(step)
        meta_copy(step, me, peer).wait_send()
        raw_copy(step, me, peer).wait_send()
        table_copy(step, me, peer).wait_send()
    for step in range(1, sources):
        peer = row_peer(step)
        table_copy(step, peer, peer).wait_recv()
        table_ref[...] += table_in[peer]
    for step in range(1, sources):
        peer = row_peer(step)

        def end_group(group, carry):
            hist_copy(step, me, peer, group).wait_send()
            hist_copy(step, peer, peer, group).wait_recv()
            return carry

        lax.fori_loop(0, groups, end_group, 0)


def on_device(binned, node_of, margin, labels, split_feature, split_bin):
    row_count, feat_count = binned.shape
    nodes = split_feature.shape[0]
    sources = lax.axis_size("rows")
    columns = lax.axis_size("feat")
    feats = feat_count // sources
    share = 2 * nodes // sources
    feat_start = lax.axis_index("feat") * feat_count
    probability = jax.nn.sigmoid(margin)
    gradient = lax.reduce_precision(probability - labels, 8, 7)
    hessian = lax.reduce_precision(probability * (1.0 - probability), 8, 7)
    node_hot = node_of[None, :] == jnp.arange(nodes, dtype=jnp.int32)[:, None]
    row_feature = jnp.sum(jnp.where(node_hot, split_feature[:, None], 0), axis=0)
    row_cut = jnp.sum(jnp.where(node_hot, split_bin[:, None], 0), axis=0)
    local = row_feature - feat_start
    binned_t = binned.T
    column_hot = jnp.arange(feat_count, dtype=jnp.int32)[:, None] == local[None, :]
    right_bits = jnp.sum(
        (column_hot & (binned_t > row_cut[None, :])).astype(jnp.int32), axis=0, keepdims=True
    )
    bins = binned_t.astype(jnp.bfloat16).reshape(sources, feats, row_count)
    meta = jnp.stack([gradient, hessian, node_of.astype(jnp.float32)])
    vmem = pl.BlockSpec(memory_space=pltpu.VMEM)
    dma = pltpu.SemaphoreType.DMA
    hist, go_right, table = pl.pallas_call(
        functools.partial(level_kernel, sources, columns, nodes, feats),
        out_shape=[
            jax.ShapeDtypeStruct((sources, feats, share, BINS), jnp.bfloat16),
            jax.ShapeDtypeStruct((1, row_count), jnp.int32),
            jax.ShapeDtypeStruct((nodes, 128), jnp.float32),
        ],
        in_specs=[vmem] * 3,
        out_specs=[vmem] * 3,
        scratch_shapes=[
            pltpu.VMEM((sources, feats, row_count), jnp.bfloat16),
            pltpu.VMEM((sources, 3, row_count), jnp.float32),
            pltpu.VMEM((columns, 1, row_count), jnp.int32),
            pltpu.VMEM((sources, nodes, 128), jnp.float32),
            pltpu.VMEM((sources, feats, row_count), jnp.float32),
            pltpu.VMEM((sources, 4 * nodes, row_count), jnp.float8_e4m3fn),
            pltpu.VMEM((feats, 4 * nodes, BINS), jnp.float32),
            pltpu.VMEM((sources, feats, share, BINS), jnp.bfloat16),
            dma((sources,)),
            dma((sources,)),
            dma((sources,)),
            dma((sources,)),
            dma((columns,)),
            dma((columns,)),
            dma((sources,)),
            dma((sources,)),
            dma((sources, feats // GROUP)),
            dma((sources, feats // GROUP)),
        ],
        compiler_params=pltpu.CompilerParams(
            collective_id=0, has_side_effects=True, vmem_limit_bytes=40 * 1024 * 1024
        ),
    )(bins, meta, right_bits)
    histogram = hist.transpose(2, 0, 1, 3).reshape(nodes // sources, 2, feat_count, BINS)
    histogram = histogram.astype(jnp.float32)

    go_right = go_right[0]
    leaf_left = -table[:, 0] / (table[:, 1] + 1.0)
    leaf_right = -(table[:, 2] - table[:, 0]) / (table[:, 3] - table[:, 1] + 1.0)
    leaf = jnp.where(go_right[None, :] == 1, leaf_right[:, None], leaf_left[:, None])
    margin_out = margin + jnp.sum(jnp.where(node_hot, leaf, 0.0), axis=0)
    child_out = 2 * node_of + go_right
    fresh = jax.nn.sigmoid(margin_out)
    grad_out = jnp.stack([fresh - labels, fresh * (1.0 - fresh)], axis=0)
    return (histogram, margin_out, child_out, grad_out)


def solution(mesh):
    in_specs = (P("rows", "feat"), P("rows"), P("rows"), P("rows"), P(), P())
    out_specs = (P("rows", None, "feat", None), P("rows"), P("rows"), P(None, "rows"))
    return jax.shard_map(
        on_device, mesh=mesh, in_specs=in_specs, out_specs=out_specs, check_vma=False
    )
```
